256 devices in a mesh: section: 8 (over x, y_hi), replica: 16 (over z, core), tensor: 2 (over y_lo).
Axes of the slice: x: 4, y: 4 (y_hi: 2, y_lo: 2; y = y_hi * 2 + y_lo), z: 8, core: 2. Of those that a mesh axis runs over, the one named last changes fastest.
Arguments:
- fresh: bfloat16 [8, 16, 16, 16, 2560], P('section', 'replica', None, None, 'tensor'), may hold values from -6 to 6
- counts: int32 [8, 16], P('section', 'replica'), may hold values from 4 to 16, as said below
- wiring: int32 [8, 16, 16, 1], P('section', 'replica'), may hold values from 0 to 15; in each aligned block of 16 rows (0 to 15, 16 to 31, ..., all dimensions but the last counted through in order) at most 2 rows name the same one
- weights: bfloat16 [8, 2560, 2560], P('section', 'tensor'), may hold values from -0.125 to 0.125
- kept: bfloat16 [8, 16, 32, 16, 2560], P('section', 'replica', None, None, 'tensor'), may hold values from -6 to 6
- upstream: bfloat16 [8, 16, 32, 16, 2560], P('section', 'replica', None, None, 'tensor'), may hold values from -6 to 6
Outputs:
- arrived: bfloat16 [8, 16, 32, 16, 2560], P('section', 'replica', None, None, 'tensor')
- returned: bfloat16 [8, 16, 16, 16, 2560], P('section', 'replica', None, None, 'tensor')
- weight_grad: float32 [8, 2560, 2560], P('section', ('tensor', 'replica'))
The draws below stay inside these ranges and needn't reach their ends.
Inputs may be any that keep to these rules, and one draw needn't show every extreme that they name: `counts`: each section has a replica with all 16 slots live and one with 4; every count is 16, 8 or 4. `wiring`: the slots of one replica name each next-section replica at most 2 times.
All inputs are finite; a program needn't handle non-finite values.
Results may differ from the reference program's by a relative error of at most 0.0034.
Values may be sent and summed in bfloat16 or wider, within the bound.
No kernel may reach another device: no remote copies, remote signals or barrier semaphores. Data moves between devices by JAX's collectives and lax.ppermute only.
A program may use at most 128 MiB of HBM per device.

```python
import math
import jax
import jax.numpy as jnp
import numpy as np
from jax import lax

F = 2560
SLOTS = 16
CAP = 2
MB = 16
SECTIONS = 8
REPLICAS = 16
RECV = 32


def draw_counts(key, part):
    key = jax.random.fold_in(key, 7)
    first_key, second_key = jax.random.split(key)
    shifts = jax.random.randint(first_key, (SECTIONS, REPLICAS), 0, 3)
    loads = jnp.right_shift(SLOTS * jnp.ones_like(shifts), shifts)
    chosen = jax.random.randint(second_key, (SECTIONS, 1), 0, REPLICAS)
    replica_index = jnp.arange(REPLICAS)[None, :]
    fewest = SLOTS // 4 * jnp.ones_like(loads)
    loads = jnp.where(replica_index == (chosen + 1) % REPLICAS, fewest, loads)
    return jnp.where(replica_index == chosen, SLOTS, loads).astype(jnp.int32)


def with_spikes(drawn, stream_key, source, target, blocks, factor):
    owner, partner = [(jnp.arange(drawn.shape[axis_at]) // (drawn.shape[axis_at] // blocks)).reshape([-1 if axis == axis_at else 1 for axis in range(drawn.ndim)]) for axis_at in (source, target)]
    chosen = jax.random.permutation(stream_key, blocks)[partner]
    strong = (owner == chosen) | (owner == (partner + blocks // 2) % blocks)
    return jnp.where(strong, factor * drawn, drawn)


def steps_of(stream_key, extent, cuts, smallest, top_value):
    factor_of, own = 1.0, jax.random.fold_in(stream_key, 6)
    for position, parts in cuts:
        steps = jnp.exp(jax.random.uniform(jax.random.fold_in(own, position), (parts,), jnp.float32, smallest / len(cuts), top_value / len(cuts)))
        factor_of = factor_of * jnp.repeat(steps, extent[position] // parts).reshape([-1 if axis == position else 1 for axis in range(len(extent))])
    return factor_of


def routed_block(own_key, own, number, rows, number_of, top, reach, lean):
    ranking = jax.random.permutation(own_key, number_of)
    crowded, usual = load_shares(number_of, rows * top, reach, lean, True), load_shares(number_of, rows * top, reach, lean, False)
    places = jnp.arange(number_of)

    def named(tallies, rotation):
        used = int((tallies > 0).sum())
        fixed = max(1, used // 4)
        moved = fixed + (places - fixed + rotation * (used - fixed)) % max(1, number_of - fixed)
        return jnp.zeros((number_of,), jnp.int32).at[ranking[jnp.where(places < fixed, places, moved)]].set(jnp.asarray(tallies, jnp.int32))

    tallies = jnp.where(number % 4 == 0, named(crowded, number // 4), named(usual, number - number // 4 - 1))
    mixed = jax.random.permutation(jax.random.fold_in(own, 3), number_of)
    giver, receiver = mixed[0:number_of // 2 * 2:2], mixed[1:number_of // 2 * 2:2]
    slack = jnp.minimum(tallies[giver] - 1, reach - tallies[receiver]) // 2
    slack = jnp.where((giver == ranking[0]) | (receiver == ranking[0]) | (tallies[receiver] == 0), 0, jnp.maximum(slack, 0))
    moved = jax.random.randint(jax.random.fold_in(own, 4), (number_of // 2,), 0, 1 << 20) % (slack + 1)
    tallies = tallies.at[giver].add(-moved).at[receiver].add(moved)
    labels = jnp.searchsorted(jnp.cumsum(tallies), jnp.arange(rows * top), side="right").astype(jnp.int32)
    listing = labels.reshape(top, rows).T
    listing = listing[jax.random.permutation(jax.random.fold_in(own, 1), rows)]
    rotation = jax.random.randint(jax.random.fold_in(own, 2), (rows, 1), 0, top)
    return jnp.take_along_axis(listing, (jnp.arange(top)[None, :] + rotation) % top, axis=1)


def load_shares(count, total, most, skew, full):
    weights = [(1 << 20) // math.isqrt(standing ** skew) + 1 for standing in range(1, count + 1)]
    largest = most if full else min(most, max(-(-total // count), total * weights[0] // sum(weights)))
    least = 1 if total - largest >= count - 1 else 0
    holding, rest = [largest] + [least] * (count - 1), total - largest - least * (count - 1)
    while rest > 0:
        free = [i for i in range(1, count) if holding[i] < largest] or [i for i in range(1, count) if holding[i] < most]
        whole, budget = sum([weights[i] for i in free]), rest
        for i in free:
            more = min(most - holding[i], max(1, budget * weights[i] // whole), rest)
            holding[i] = holding[i] + more
            rest = rest - more
    return np.array(holding)


def bell_draw(stream_key, shape, deviation, most, cuts=(), kind=jnp.bfloat16):
    entries = jax.random.normal(stream_key, shape, jnp.float32) * deviation
    if len(cuts) > 0:
        entries = steps_of(stream_key, shape, cuts, -0.22, 0.18) * entries
    return jnp.clip(entries, min=-most, max=most).astype(kind)


def noise_with(key, shape, width, bound, cuts, heavy, held_as=jnp.bfloat16):
    values = width * jax.random.normal(key, shape, jnp.float32)
    if cuts:
        values = values * steps_of(key, shape, cuts, -0.22, 0.18)
    return jnp.clip(with_spikes(values, jax.random.fold_in(key, 3), *heavy), -bound, bound).astype(held_as)


def setup_inputs(seed: int = 0) -> dict:
    streams_of = jax.random.split(jax.random.key(seed), 7)
    fresh = bell_draw(streams_of[0], (SECTIONS, REPLICAS, SLOTS, MB, F), 1.0, 6.0, ((0, 8), (1, 16), (4, 2)))
    counts = draw_counts(jax.random.fold_in(streams_of[6], 71), 0)
    wiring_keys = jax.random.split(jax.random.fold_in(streams_of[2], 1), SECTIONS * REPLICAS * SLOTS // SLOTS)
    wiring_turns = jax.random.permutation(jax.random.fold_in(streams_of[2], 3), SECTIONS * REPLICAS * SLOTS // SLOTS)
    wiring = jax.vmap(lambda own, number: routed_block(jax.random.fold_in(streams_of[2], 2), own, number, SLOTS, REPLICAS, 1, CAP, 2))(wiring_keys, wiring_turns).reshape((SECTIONS, REPLICAS, SLOTS, 1))
    weights = bell_draw(streams_of[3], (SECTIONS, F, F), F ** -0.5, 0.125, ((0, 8), (1, 2)))
    kept = noise_with(streams_of[4], (SECTIONS, REPLICAS, RECV, MB, F), 1.0, 6.0, ((0, 8), (1, 16), (4, 2)), (1, 4, 16, 2.0))
    upstream = bell_draw(streams_of[5], (SECTIONS, REPLICAS, RECV, MB, F), 1.0, 6.0, ((0, 8), (1, 16), (4, 2)))
    return {"fresh": fresh, "counts": counts, "wiring": wiring, "weights": weights, "kept": kept, "upstream": upstream}


def silu_slope(values):
    gate_value = jax.nn.sigmoid(values)
    return gate_value * (1.0 + values * (1.0 - gate_value))


def selectors(wiring_section):
    target = wiring_section[:, :, 0]
    slot_index = jnp.arange(SLOTS)
    same_target = target[:, :, None] == target[:, None, :]
    earlier = slot_index[None, :] < slot_index[:, None]
    pair_rank = jnp.sum(same_target & earlier[None], axis=2).astype(jnp.int32)
    buffer_slot = target * CAP + pair_rank
    picked = buffer_slot[:, :, None] == jnp.arange(REPLICAS * CAP)[None, None, :]
    return picked.astype(jnp.float32).reshape(REPLICAS, SLOTS, REPLICAS, CAP)


def reference(fresh, counts, wiring, weights, kept, upstream):
    arrived_list = [jnp.zeros((REPLICAS, RECV, MB, F), jnp.bfloat16)]
    marks_list = [jnp.zeros((REPLICAS, RECV), jnp.float32)]
    picks = []
    for section_id in range(SECTIONS):
        inputs = fresh[section_id].reshape(-1, F)
        forward_z = jnp.dot(inputs, weights[section_id], preferred_element_type=jnp.float32)
        live_slots = (jnp.arange(SLOTS)[None, :] < counts[section_id][:, None]).astype(jnp.float32)
        summed = inputs.astype(jnp.float32) + jax.nn.silu(forward_z)
        outputs = (summed.reshape(REPLICAS, SLOTS, MB, F) * live_slots[:, :, None, None]).astype(jnp.bfloat16)
        picked = selectors(wiring[section_id])
        picks.append(picked)
        if section_id + 1 < SECTIONS:
            packed = jnp.einsum("rjwc,rjmf->wrcmf", picked, outputs.astype(jnp.float32))
            arrived_list.append(packed.reshape(REPLICAS, RECV, MB, F).astype(jnp.bfloat16))
            flags = jnp.einsum("rjwc,rj->wrc", picked, live_slots)
            marks_list.append(flags.reshape(REPLICAS, RECV))
    returned_list = []
    grad_list = []
    for section_id in range(SECTIONS):
        stored = kept[section_id].reshape(-1, F)
        backward_z = jnp.dot(stored, weights[section_id], preferred_element_type=jnp.float32)
        grads_in = upstream[section_id].reshape(-1, F).astype(jnp.float32)
        mask_rows = jnp.broadcast_to(marks_list[section_id][:, :, None], (REPLICAS, RECV, MB)).reshape(-1, 1)
        gate_grad = (grads_in * silu_slope(backward_z) * mask_rows).astype(jnp.bfloat16)
        back_terms = lax.dot_general(gate_grad, weights[section_id], (((1,), (1,)), ((), ())), preferred_element_type=jnp.float32)
        input_grad = ((grads_in + back_terms) * mask_rows).astype(jnp.bfloat16)
        grad_list.append(lax.dot_general(stored, gate_grad, (((0,), (0,)), ((), ())), preferred_element_type=jnp.float32))
        if section_id > 0:
            back_buf = input_grad.reshape(REPLICAS, REPLICAS, CAP, MB, F).astype(jnp.float32)
            slot_grads = jnp.einsum("rjwc,wrcmf->rjmf", picks[section_id - 1], back_buf)
            returned_list.append(slot_grads.astype(jnp.bfloat16))
    returned_list.append(jnp.zeros((REPLICAS, SLOTS, MB, F), jnp.bfloat16))
    return jnp.stack(arrived_list), jnp.stack(returned_list), jnp.stack(grad_list)
```

```python
import jax
import jax.numpy as jnp
from jax import lax
from jax.experimental import pallas as pl
from jax.experimental.pallas import tpu as pltpu
from jax.sharding import PartitionSpec as P

Z_SCALE = 64.0
Z_BACK = 1.0 / 64.0
TILE = 256
VMEM_BYTES = 40 * 1024 * 1024


def shift(block, axis, distance):
    devices = range(lax.axis_size(axis))
    route = [(i, i + distance) for i in devices if i + distance in devices]
    return lax.ppermute(block, axis, route)


def swap_tensor(block):
    return lax.ppermute(block, "tensor", [(0, 1), (1, 0)])


def swap_core(block):
    return lax.ppermute(block, "replica", [(r, r ^ 1) for r in range(lax.axis_size("replica"))])


def round_chips(block, distance):
    size = lax.axis_size("replica")
    return lax.ppermute(block, "replica", [(r, (r + 2 * distance) % size) for r in range(size)])


def params():
    return pltpu.CompilerParams(vmem_limit_bytes=VMEM_BYTES)


def cost(flops, moved):
    return pl.CostEstimate(flops=flops, bytes_accessed=moved, transcendentals=0)


def project_body(half_ref, x_ref, w_ref, o_ref):
    o_ref[...] = jnp.dot(x_ref[...], w_ref[...], preferred_element_type=jnp.float32)


def project(x, weight, half):
    rows, depth = x.shape
    width = weight.shape[1] // 2
    tiles = width // TILE
    return pl.pallas_call(
        project_body,
        grid_spec=pltpu.PrefetchScalarGridSpec(
            num_scalar_prefetch=1,
            grid=(tiles,),
            in_specs=[
                pl.BlockSpec((rows, depth), lambda j, h: (0, 0)),
                pl.BlockSpec((depth, TILE), lambda j, h: (0, h[0] * tiles + j)),
            ],
            out_specs=pl.BlockSpec((rows, TILE), lambda j, h: (0, j)),
        ),
        out_shape=jax.ShapeDtypeStruct((rows, width), jnp.float32),
        compiler_params=params(),
        cost_estimate=cost(2 * rows * depth * width, 2 * depth * width + 4 * rows * width),
    )(half, x, weight)


def back_body(half_ref, own_ref, nbr_ref, wo_ref, wn_ref, up_ref, mask_ref, o_ref):
    dims = (((1,), (1,)), ((), ()))
    terms = lax.dot_general(own_ref[...], wo_ref[...], dims, preferred_element_type=jnp.float32)
    terms += lax.dot_general(nbr_ref[...], wn_ref[...], dims, preferred_element_type=jnp.float32)
    o_ref[...] = ((up_ref[...].astype(jnp.float32) + terms) * mask_ref[...]).astype(jnp.bfloat16)


def back_project(own, nbr, weight, half, up, mask):
    rows, depth = own.shape
    width = weight.shape[0]
    return pl.pallas_call(
        back_body,
        grid_spec=pltpu.PrefetchScalarGridSpec(
            num_scalar_prefetch=1,
            grid=(width // TILE,),
            in_specs=[
                pl.BlockSpec((rows, depth), lambda j, h: (0, 0)),
                pl.BlockSpec((rows, depth), lambda j, h: (0, 0)),
                pl.BlockSpec((TILE, depth), lambda j, h: (j, h[0])),
                pl.BlockSpec((TILE, depth), lambda j, h: (j, 1 - h[0])),
                pl.BlockSpec((rows, TILE), lambda j, h: (0, j)),
                pl.BlockSpec((rows, 1), lambda j, h: (0, 0)),
            ],
            out_specs=pl.BlockSpec((rows, TILE), lambda j, h: (0, j)),
        ),
        out_shape=jax.ShapeDtypeStruct((rows, width), jnp.bfloat16),
        compiler_params=params(),
        cost_estimate=cost(4 * rows * depth * width, 4 * depth * width + 4 * rows * width),
    )(half, own, nbr, weight, weight, up, mask)


def outer_body(other_ref, mine_ref, ga_ref, gb_ref, send_ref, keep_ref):
    rows = ga_ref.shape[0]
    for lhs, out in ((other_ref, send_ref), (mine_ref, keep_ref)):
        out[...] = jnp.dot(lhs[:, :rows], ga_ref[...], preferred_element_type=jnp.float32) + jnp.dot(
            lhs[:, rows:], gb_ref[...], preferred_element_type=jnp.float32
        )


def outer_sum(other, mine, gate_a, gate_b):
    depth, rows = other.shape
    width = gate_a.shape[1]
    part = gate_a.shape[0]
    out = jax.ShapeDtypeStruct((depth, width), jnp.float32)
    return pl.pallas_call(
        outer_body,
        grid=(width // TILE,),
        in_specs=[
            pl.BlockSpec((depth, rows), lambda j: (0, 0)),
            pl.BlockSpec((depth, rows), lambda j: (0, 0)),
            pl.BlockSpec((part, TILE), lambda j: (0, j)),
            pl.BlockSpec((part, TILE), lambda j: (0, j)),
        ],
        out_specs=[pl.BlockSpec((depth, TILE), lambda j: (0, j))] * 2,
        out_shape=[out, out],
        compiler_params=params(),
        cost_estimate=cost(4 * rows * depth * width, 8 * depth * width),
    )(other, mine, gate_a, gate_b)


def pick_body(index_ref, x_ref, o_ref):
    def step(i, carry):
        source = index_ref[i]
        block = x_ref[jnp.maximum(source, 0)]
        o_ref[i] = jnp.where(source >= 0, block, jnp.zeros_like(block))
        return carry

    lax.fori_loop(0, o_ref.shape[0], step, 0)


def pick(index, x):
    count = index.shape[0]
    return pl.pallas_call(
        pick_body,
        in_specs=[
            pl.BlockSpec(memory_space=pltpu.SMEM),
            pl.BlockSpec(memory_space=pltpu.VMEM),
        ],
        out_specs=pl.BlockSpec(memory_space=pltpu.VMEM),
        out_shape=jax.ShapeDtypeStruct((count,) + x.shape[1:], x.dtype),
        compiler_params=params(),
        cost_estimate=cost(0, 2 * 2 * count * x.shape[1] * x.shape[2]),
    )(index, x)


def ring_sum(keep, send, scale):
    chips = lax.axis_size("replica") // 2
    me = lax.axis_index("replica") // 2
    got = swap_core(send)

    def term(offset):
        at = (me + offset + chips) % chips
        first = lax.dynamic_index_in_dim(keep, at, 0, keepdims=False)
        return (first + lax.dynamic_index_in_dim(got, at, 0, keepdims=False)) * scale

    down = up = None
    far = chips // 2
    for k in range(far, 0, -1):
        s = term(-k)
        s = s if down is None else s + down.astype(jnp.float32)
        down = round_chips(s.astype(jnp.float16), -1)
        if k < far:
            s = term(k)
            s = s if up is None else s + up.astype(jnp.float32)
            up = round_chips(s.astype(jnp.float16), 1)
    total = term(0) + down.astype(jnp.float32) + up.astype(jnp.float32)
    return total * (1.0 / scale)


def local(fresh, counts, wiring, weights, kept, upstream):
    replicas = lax.axis_size("replica")
    chips = replicas // 2
    slots, tokens, width = fresh.shape[2:]
    recv = kept.shape[2]
    cap = recv // replicas
    cut = tokens // 2
    weight = weights[0]
    own = lax.axis_index("tensor").astype(jnp.int32)[None]
    nbr = 1 - own
    core = lax.axis_index("replica") % 2

    plan = jnp.concatenate([wiring[0, 0, :, 0], counts[0]])[None]
    plan = shift(plan, "section", 1)[0]
    target, count = plan[:slots], plan[slots]
    slot = jnp.arange(slots)
    same = target[:, None] == target[None, :]
    rank = jnp.sum(same & (slot[None, :] < slot[:, None]), axis=1).astype(jnp.int32)
    place = target * cap + rank
    hit = (place[None, :] == jnp.arange(recv)[:, None]) & (slot < count)[None, :]
    source = (jnp.sum(jnp.where(hit, slot[None, :] + 1, 0), axis=1) - 1).astype(jnp.int32)
    flags = jnp.any(hit, axis=1).astype(jnp.bfloat16).reshape(replicas, cap)
    tops = jnp.stack([jnp.max(jnp.abs(kept)), jnp.max(jnp.abs(upstream))])
    tops = jnp.broadcast_to(tops[None], (replicas, 2))
    told = lax.all_to_all(
        jnp.concatenate([flags, tops], axis=1), "replica", split_axis=0, concat_axis=0, tiled=True
    ).astype(jnp.float32)
    marks = told[:, :cap].reshape(recv)
    terms = 1.11 * replicas * recv * tokens
    top_kept, top_own = jnp.max(told[:, cap]), jnp.max(told[:, cap + 1])
    top_nbr = swap_tensor(top_own[None])[0]
    scale_own = 60000.0 / (terms * jnp.maximum(top_kept * top_own, 1e-25))
    scale_nbr = 60000.0 / (terms * jnp.maximum(top_kept * top_nbr, 1e-25))
    mask = jnp.broadcast_to(marks[:, None], (recv, cut)).reshape(recv * cut, 1)

    inputs = fresh[0, 0].reshape(slots * tokens, width)
    away = (project(inputs, weight, nbr) * Z_SCALE).astype(jnp.float16)
    forward_away = swap_tensor(away)
    halves = lambda v: [
        v[0, 0, :, h * cut : (h + 1) * cut].reshape(recv * cut, width) for h in range(2)
    ]
    kept_parts = halves(kept)
    up_parts = halves(upstream)
    stored = jnp.concatenate(kept_parts, axis=0)
    back_away = (project(stored, weight, nbr) * Z_SCALE).astype(jnp.float16)
    rows = recv * cut
    back_got = [swap_tensor(back_away[:rows]), swap_tensor(back_away[rows:])]
    forward_own = project(inputs, weight, own)
    back_own = project(stored, weight, own)
    turned = stored.T.reshape(chips, 2, width // replicas, 2 * rows)
    mine = lax.dynamic_index_in_dim(turned, core, 1, keepdims=False).reshape(width // 2, 2 * rows)
    other = lax.dynamic_index_in_dim(turned, 1 - core, 1, keepdims=False)
    other = other.reshape(width // 2, 2 * rows)

    forward_z = forward_own + forward_away.astype(jnp.float32) * Z_BACK
    live = (slot < counts[0, 0]).astype(jnp.float32)
    live_rows = jnp.broadcast_to(live[:, None], (slots, tokens)).reshape(slots * tokens, 1)
    outputs = ((inputs.astype(jnp.float32) + jax.nn.silu(forward_z)) * live_rows).astype(
        jnp.bfloat16
    )
    outputs = shift(outputs.reshape(slots, tokens, width), "section", 1)
    packed = pick(source, outputs).reshape(replicas, cap, tokens, width)
    arrived = lax.all_to_all(packed, "replica", split_axis=0, concat_axis=0, tiled=True)

    gates, gates_nbr, returned = [], [], []
    for h in range(2):
        z = back_own[h * rows : (h + 1) * rows] + back_got[h].astype(jnp.float32) * Z_BACK
        g = jax.nn.sigmoid(z)
        slope = g * (1.0 + z * (1.0 - g))
        gate = (up_parts[h].astype(jnp.float32) * slope * mask).astype(jnp.bfloat16)
        gates.append(gate)
        gates_nbr.append(swap_tensor(gate))
    for h in range(2):
        grad = back_project(gates[h], gates_nbr[h], weight, own, up_parts[h], mask)
        grad = grad.reshape(replicas, cap, cut, width)
        back = lax.all_to_all(grad, "replica", split_axis=0, concat_axis=0, tiled=True)
        chosen = pick(place, back.reshape(recv, cut, width))
        returned.append(shift(chosen, "section", -1))
    returned = jnp.concatenate(returned, axis=1)

    block = (chips, width // replicas, width)
    send, keep = outer_sum(other, mine, gates[0], gates[1])
    sum_own = ring_sum(keep.reshape(block), send.reshape(block), scale_own)
    send, keep = outer_sum(other, mine, gates_nbr[0], gates_nbr[1])
    sum_nbr = ring_sum(keep.reshape(block), send.reshape(block), scale_nbr)
    first = own[0] == 0
    weight_grad = jnp.concatenate(
        [jnp.where(first, sum_own, sum_nbr), jnp.where(first, sum_nbr, sum_own)], axis=1
    )
    return (
        arrived.reshape(1, 1, recv, tokens, width),
        returned[None, None],
        weight_grad[None],
    )


def solution(mesh):
    placed = (
        P("section", "replica", None, None, "tensor"),
        P("section", "replica"),
        P("section", "replica", None, None),
        P("section", "tensor", None),
        P("section", "replica", None, None, "tensor"),
        P("section", "replica", None, None, "tensor"),
    )
    return jax.shard_map(
        local,
        mesh=mesh,
        in_specs=placed,
        out_specs=(
            P("section", "replica", None, None, "tensor"),
            P("section", "replica", None, None, "tensor"),
            P("section", ("tensor", "replica"), None),
        ),
        check_vma=False,
    )
```

```python
import jax
import jax.numpy as jnp
from jax import lax
from jax.experimental import pallas as pl
from jax.experimental.pallas import tpu as pltpu
from jax.sharding import PartitionSpec as P

Z_SCALE = 64.0
Z_BACK = 1.0 / 64.0
TILE = 256
VMEM_BYTES = 24 * 1024 * 1024

def shift(block, axis, distance):
    devices = range(lax.axis_size(axis))
    route = [(i, i + distance) for i in devices if i + distance in devices]
    return lax.ppermute(block, axis, route)


def swap_tensor(block):
    return lax.ppermute(block, "tensor", [(0, 1), (1, 0)])


def swap_core(block):
    return lax.ppermute(block, "replica", [(r, r ^ 1) for r in range(lax.axis_size("replica"))])


def round_chips(block, distance):
    size = lax.axis_size("replica")
    return lax.ppermute(block, "replica", [(r, (r + 2 * distance) % size) for r in range(size)])


def shaped(shape, dtype):
    return jax.ShapeDtypeStruct(shape, dtype)


def in_hbm(x):
    return pltpu.with_memory_space_constraint(x, pltpu.HBM)


def kernel(body, out_shape, operands, spaces, scratch=(), out_space=pltpu.VMEM, aliases=None):
    single = not isinstance(out_shape, list)
    spec = pl.BlockSpec(memory_space=out_space)
    return pl.pallas_call(
        body,
        in_specs=[pl.BlockSpec(memory_space=space) for space in spaces],
        out_specs=spec if single else [spec] * len(out_shape),
        out_shape=out_shape,
        scratch_shapes=list(scratch),
        input_output_aliases=aliases or {},
        compiler_params=pltpu.CompilerParams(vmem_limit_bytes=VMEM_BYTES),
        cost_estimate=pl.CostEstimate(flops=1024, bytes_accessed=1024, transcendentals=0),
    )(*operands)


def project_body(half_ref, x_ref, w_ref, o_ref, held, sems, *out):
    tiles, _, tile = held.shape
    base = half_ref[0] * (tiles * tile)

    def fetch(j):
        at = pl.multiple_of(base + j * tile, tile)
        return pltpu.make_async_copy(w_ref.at[:, pl.ds(at, tile)], held.at[j], sems.at[j])

    for j in range(tiles):
        fetch(j).start()

    def step(j, carry):
        fetch(j).wait()
        z = jnp.dot(x_ref[...], held[j], preferred_element_type=jnp.float32)
        if out:
            out[0][j] = z
            store(j).start()
        else:
            o_ref[:, pl.ds(pl.multiple_of(j * tile, tile), tile)] = z
        return carry

    def store(j):
        at = pl.ds(pl.multiple_of(j * tile, tile), tile)
        return pltpu.make_async_copy(out[0].at[j], o_ref.at[:, at], out[1].at[j])

    lax.fori_loop(0, tiles, step, 0)
    if out:
        for j in range(tiles):
            store(j).wait()


def project(x, weight, half, keep=False):
    rows, depth = x.shape
    width = weight.shape[1] // 2
    tiles = width // TILE
    scratch = [pltpu.VMEM((tiles, depth, TILE), weight.dtype), pltpu.SemaphoreType.DMA((tiles,))]
    if keep:
        scratch += [pltpu.VMEM((tiles, rows, TILE), jnp.float32), pltpu.SemaphoreType.DMA((tiles,))]
    return kernel(
        project_body,
        pltpu.HBM((rows, width), jnp.float32) if keep else shaped((rows, width), jnp.float32),
        (half, x, in_hbm(weight)),
        (pltpu.SMEM, pltpu.VMEM, pl.ANY),
        scratch,
        pltpu.HBM if keep else pltpu.VMEM,
    )


def back_body(row, half_ref, own_ref, nbr_ref, w_ref, up_ref, mask_ref, *rest):
    o_ref, held, sems, grads, out_sems = rest[-5:]
    tiles, tile, _ = held.shape
    rows, depth = own_ref.shape
    own_at = pl.multiple_of(half_ref[0] * depth, tile)
    nbr_at = pl.multiple_of((1 - half_ref[0]) * depth, tile)
    dims = (((1,), (1,)), ((), ()))
    here = pl.ds(row, rows)

    def fetch(j):
        at = pl.multiple_of(j * tile, tile)
        return pltpu.make_async_copy(w_ref.at[pl.ds(at, tile)], held.at[j], sems.at[j])

    def store(j):
        at = pl.ds(pl.multiple_of(j * tile, tile), tile)
        return pltpu.make_async_copy(grads.at[j], o_ref.at[here, at], out_sems.at[j])

    for j in range(tiles):
        fetch(j).start()

    def step(j, carry):
        fetch(j).wait()
        at = pl.ds(pl.multiple_of(j * tile, tile), tile)
        terms = lax.dot_general(
            own_ref[...], held[j, :, pl.ds(own_at, depth)], dims, preferred_element_type=jnp.float32
        )
        terms += lax.dot_general(
            nbr_ref[...], held[j, :, pl.ds(nbr_at, depth)], dims, preferred_element_type=jnp.float32
        )
        up = up_ref[here, at].astype(jnp.float32)
        grads[j] = ((up + terms) * mask_ref[here, :]).astype(jnp.bfloat16)
        store(j).start()
        return carry

    lax.fori_loop(0, tiles, step, 0)
    for j in range(tiles):
        store(j).wait()


def back_project(own, nbr, weight, half, up, mask, row, before=None):
    width = weight.shape[0]
    tiles = width // TILE
    operands = (half, own, nbr, in_hbm(weight), up, mask)
    spaces = (pltpu.SMEM, pltpu.VMEM, pltpu.VMEM, pl.ANY, pltpu.VMEM, pltpu.VMEM)
    aliases = {}
    if before is not None:
        aliases = {len(operands): 0}
        operands, spaces = operands + (before,), spaces + (pl.ANY,)

    def body(*refs):
        back_body(row, *refs)

    return kernel(
        body,
        pltpu.HBM(up.shape, jnp.bfloat16),
        operands,
        spaces,
        [
            pltpu.VMEM((tiles, TILE, 2 * width), weight.dtype),
            pltpu.SemaphoreType.DMA((tiles,)),
            pltpu.VMEM((tiles, own.shape[0], TILE), jnp.bfloat16),
            pltpu.SemaphoreType.DMA((tiles,)),
        ],
        pltpu.HBM,
        aliases,
    )


def outer_body(other_ref, mine_ref, ga_ref, gb_ref, mask_ref, send_ref, keep_ref, sent, kept, sems):
    tiles, _, tile = kept.shape
    rows = ga_ref.shape[0]

    def store(j, i):
        at = pl.ds(pl.multiple_of(j * tile, tile), tile)
        out, ref = ((sent, send_ref), (kept, keep_ref))[i]
        return pltpu.make_async_copy(out.at[j], ref.at[:, at], sems.at[j, i])

    def step(j, carry):
        at = pl.ds(pl.multiple_of(j * tile, tile), tile)
        ga = (ga_ref[:, at].astype(jnp.float32) * mask_ref[:rows]).astype(jnp.bfloat16)
        gb = (gb_ref[:, at].astype(jnp.float32) * mask_ref[rows:]).astype(jnp.bfloat16)
        for i, lhs, out in ((0, other_ref, sent), (1, mine_ref, kept)):
            total = jnp.dot(lhs[:, :rows], ga, preferred_element_type=jnp.float32)
            total += jnp.dot(lhs[:, rows:], gb, preferred_element_type=jnp.float32)
            out[j] = total.astype(out.dtype)
            store(j, i).start()
        return carry

    lax.fori_loop(0, tiles, step, 0)
    for j in range(tiles):
        for i in range(2):
            store(j, i).wait()


def outer_sum(other, mine, gate_a, gate_b, mask):
    depth, width = other.shape[0], gate_a.shape[1]
    tiles = width // TILE
    return kernel(
        outer_body,
        [pltpu.HBM((depth, width), jnp.bfloat16), pltpu.HBM((depth, width), jnp.float32)],
        (other, mine, gate_a, gate_b, mask),
        (pltpu.VMEM,) * 5,
        [
            pltpu.VMEM((tiles, depth, TILE), jnp.bfloat16),
            pltpu.VMEM((tiles, depth, TILE), jnp.float32),
            pltpu.SemaphoreType.DMA((tiles, 2)),
        ],
        pltpu.HBM,
    )


def pick_body(index_ref, x_ref, o_ref):
    def step(i, carry):
        source = index_ref[i]
        block = x_ref[jnp.maximum(source, 0)]
        o_ref[i] = jnp.where(source >= 0, block, jnp.zeros_like(block))
        return carry

    lax.fori_loop(0, o_ref.shape[0], step, 0)


def pick(index, x):
    shape = shaped((index.shape[0],) + x.shape[1:], x.dtype)
    return kernel(pick_body, shape, (index, x), (pltpu.SMEM, pltpu.VMEM))


class Order:
    def __init__(self):
        self.last = None

    def tie(self, *arrays):
        if self.last is None:
            return arrays
        return lax.optimization_barrier(arrays + (self.last,))[:-1]

    def mark(self, array):
        self.last = array
        return array

    def here(self, *arrays):
        arrays = self.tie(*arrays)
        self.last = arrays[0]
        return arrays


class Ring:
    def __init__(self, order, keep, send):
        self.order, self.keep = order, keep
        self.got = swap_core(send)
        self.down = self.up = None
        self.next = lax.axis_size("replica") // 4

    def term(self, keep, got, offset, extra):
        chips = lax.axis_size("replica") // 2
        at = (lax.axis_index("replica") // 2 + offset + chips) % chips
        s = lax.dynamic_index_in_dim(keep, at, 0, keepdims=False)
        s = s + lax.dynamic_index_in_dim(got, at, 0, keepdims=False).astype(jnp.float32)
        return s if extra is None else s + extra.astype(jnp.float32)

    def round(self):
        k = self.next
        far = lax.axis_size("replica") // 4
        held = [self.keep, self.got] + [v for v in (self.down, self.up) if v is not None]
        held = list(self.order.tie(*held))
        self.keep, self.got = held[:2]
        cut = self.keep.shape[-1] // 2
        if k == far:
            sent = self.term(self.keep, self.got, k, None).astype(jnp.bfloat16)
            self.order.mark(sent)
            self.down = round_chips(sent[:, :cut], -1)
            self.up = round_chips(sent[:, cut:], 1)
        elif k == 0:
            total = self.term(self.keep, self.got, 0, held[2]) + held[3].astype(jnp.float32)
            return self.order.mark(total)
        else:
            down, up = held[2:]
            if k == far - 1:
                down = jnp.pad(down, ((0, 0), (0, cut)))
                up = jnp.pad(up, ((0, 0), (cut, 0)))
            sent = self.term(self.keep, self.got, -k, down).astype(jnp.bfloat16)
            self.down = round_chips(sent, -1)
            sent = self.term(self.keep, self.got, k, up).astype(jnp.bfloat16)
            self.up = round_chips(sent, 1)
            self.order.mark(sent)
        self.next = k - 1


def local(fresh, counts, wiring, weights, kept, upstream):
    replicas = lax.axis_size("replica")
    chips = replicas // 2
    slots, tokens, width = fresh.shape[2:]
    recv = kept.shape[2]
    cap = recv // replicas
    rows = recv * tokens // 2
    weight = weights[0]
    inputs = fresh[0, 0].reshape(slots * tokens, width)
    stored = kept[0, 0].reshape(2 * rows, width)
    up = upstream[0, 0].reshape(2 * rows, width)
    own = lax.axis_index("tensor").astype(jnp.int32)[None]
    nbr = 1 - own
    core = lax.axis_index("replica") % 2
    order = Order()

    back_nbr = order.mark(project(stored, weight, nbr))

    def send_half(h):
        (x,) = order.tie(back_nbr)
        sent = (x[h * rows : (h + 1) * rows] * Z_SCALE).astype(jnp.float16)
        return swap_tensor(order.mark(sent))

    back_got = [send_half(0)]
    (words,) = order.tie(jnp.concatenate([wiring[0, 0, :, 0], counts[0]])[None])
    plan = shift(order.mark(words), "section", 1)[0]
    back_got.append(send_half(1))

    (x,) = order.tie(stored)
    back_own = order.mark(project(x, weight, own, True))
    (x,) = order.tie(stored)
    turned = x.T.reshape(chips, 2, width // replicas, 2 * rows)
    mine = lax.dynamic_index_in_dim(turned, core, 1, keepdims=False).reshape(width // 2, 2 * rows)
    other = lax.dynamic_index_in_dim(turned, 1 - core, 1, keepdims=False)
    other = order.mark(other.reshape(width // 2, 2 * rows))

    def gate_half(h):
        here = slice(h * rows, (h + 1) * rows)
        z_own, z_got, u = order.tie(back_own, back_got[h], up)
        z = z_own[here] + z_got.astype(jnp.float32) * Z_BACK
        g = jax.nn.sigmoid(z)
        slope = g * (1.0 + z * (1.0 - g))
        return order.mark((u[here].astype(jnp.float32) * slope).astype(jnp.bfloat16))

    def back_half(h, before=None):
        gate, got, u = order.tie(gates[h], gates_nbr[h], up)
        return order.mark(back_project(gate, got, weight, own, u, mask, h * rows, before))

    def across(block):
        return lax.all_to_all(block, "replica", split_axis=0, concat_axis=0, tiled=True)

    def ring_of(first, second):
        first, second = order.tie(first, second)
        send, keep = outer_sum(other, mine, first, second, mask)
        order.mark(keep)
        shape = (chips, width // replicas, width)
        return Ring(order, keep.reshape(shape), send.reshape(shape))

    gates = [gate_half(0)]
    gates_nbr = [swap_tensor(gates[0])]

    (plan,) = order.tie(plan)
    target, count = plan[:slots], plan[slots]
    slot = jnp.arange(slots)
    same = target[:, None] == target[None, :]
    rank = jnp.sum(same & (slot[None, :] < slot[:, None]), axis=1).astype(jnp.int32)
    place = target * cap + rank
    hit = (place[None, :] == jnp.arange(recv)[:, None]) & (slot < count)[None, :]
    source = (jnp.sum(jnp.where(hit, slot[None, :] + 1, 0), axis=1) - 1).astype(jnp.int32)
    flags = order.mark((source >= 0).astype(jnp.bfloat16).reshape(replicas, cap))
    told = across(flags)
    gates.append(gate_half(1))
    gates_nbr.append(swap_tensor(gates[1]))
    (told,) = order.tie(told)
    marks = told.reshape(recv).astype(jnp.float32)
    mask = order.mark(jnp.broadcast_to(marks[:, None], (recv, tokens)).reshape(2 * rows, 1))

    (x,) = order.tie(inputs)
    sent = order.mark((project(x, weight, nbr) * Z_SCALE).astype(jnp.float16))
    forward_got = swap_tensor(sent)
    (x,) = order.tie(inputs)
    forward_own = order.mark(project(x, weight, own, True))

    grads = back_half(0)
    ring_own = ring_of(gates[0], gates[1])
    grads = back_half(1, grads)
    back = across(grads.reshape(replicas, cap, tokens, width))

    forward_own, forward_got, x = order.tie(forward_own, forward_got, inputs)
    forward_z = forward_own + forward_got.astype(jnp.float32) * Z_BACK
    live = (slot < counts[0, 0]).astype(jnp.float32)
    live_rows = jnp.broadcast_to(live[:, None], (slots, tokens)).reshape(slots * tokens, 1)
    outputs = ((x.astype(jnp.float32) + jax.nn.silu(forward_z)) * live_rows).astype(jnp.bfloat16)
    order.mark(outputs)
    outputs = shift(outputs.reshape(slots, tokens, width), "section", 1)

    ring_nbr = ring_of(gates_nbr[0], gates_nbr[1])
    ring_own.round()
    ring_nbr.round()
    (outputs,) = order.tie(outputs)
    packed = order.mark(pick(source, outputs))
    arrived = across(packed.reshape(replicas, cap, tokens, width))
    (back,) = order.tie(back)
    returned = order.mark(pick(place, back.reshape(recv, tokens, width)))
    returned = shift(returned, "section", -1)
    ring_own.round()
    ring_nbr.round()
    ring_own.round()
    ring_nbr.round()
    ring_own.round()
    ring_nbr.round()
    sum_own = ring_own.round()
    sum_nbr = ring_nbr.round()
    zero = jnp.zeros((), jnp.int32)
    weight_grad = jnp.zeros((width // replicas, 2 * width), jnp.float32)
    weight_grad = lax.dynamic_update_slice(weight_grad, sum_own, (zero, own[0] * width))
    weight_grad = lax.dynamic_update_slice(weight_grad, sum_nbr, (zero, nbr[0] * width))
    return (
        arrived.reshape(1, 1, recv, tokens, width),
        returned[None, None],
        weight_grad[None],
    )


def solution(mesh):
    placed = (
        P("section", "replica", None, None, "tensor"),
        P("section", "replica"),
        P("section", "replica", None, None),
        P("section", "tensor", None),
        P("section", "replica", None, None, "tensor"),
        P("section", "replica", None, None, "tensor"),
    )
    return jax.shard_map(
        local,
        mesh=mesh,
        in_specs=placed,
        out_specs=(
            P("section", "replica", None, None, "tensor"),
            P("section", "replica", None, None, "tensor"),
            P("section", ("tensor", "replica"), None),
        ),
        check_vma=False,
    )
```

```python
import jax
import jax.numpy as jnp
from jax import lax
from jax.experimental import pallas as pl
from jax.experimental.pallas import tpu as pltpu
from jax.sharding import PartitionSpec as P

Z_SCALE = 64.0
Z_BACK = 1.0 / 64.0
TILE = 256
VMEM_BYTES = 24 * 1024 * 1024

def shift(block, axis, distance):
    devices = range(lax.axis_size(axis))
    route = [(i, i + distance) for i in devices if i + distance in devices]
    return lax.ppermute(block, axis, route)


def swap_tensor(block):
    return lax.ppermute(block, "tensor", [(0, 1), (1, 0)])


def swap_core(block):
    return lax.ppermute(block, "replica", [(r, r ^ 1) for r in range(lax.axis_size("replica"))])


def round_chips(block, distance):
    size = lax.axis_size("replica")
    return lax.ppermute(block, "replica", [(r, (r + 2 * distance) % size) for r in range(size)])


def shaped(shape, dtype):
    return jax.ShapeDtypeStruct(shape, dtype)


def in_hbm(x):
    return pltpu.with_memory_space_constraint(x, pltpu.HBM)


def kernel(body, out_shape, operands, spaces, scratch=(), out_space=pltpu.VMEM, aliases=None):
    single = not isinstance(out_shape, list)
    spec = pl.BlockSpec(memory_space=out_space)
    return pl.pallas_call(
        body,
        in_specs=[pl.BlockSpec(memory_space=space) for space in spaces],
        out_specs=spec if single else [spec] * len(out_shape),
        out_shape=out_shape,
        scratch_shapes=list(scratch),
        input_output_aliases=aliases or {},
        compiler_params=pltpu.CompilerParams(vmem_limit_bytes=VMEM_BYTES),
        cost_estimate=pl.CostEstimate(flops=1024, bytes_accessed=1024, transcendentals=0),
    )(*operands)


def project_body(half_ref, x_ref, w_ref, o_ref, held, sems, *out):
    tiles, _, tile = held.shape
    base = half_ref[0] * (tiles * tile)

    def fetch(j):
        at = pl.multiple_of(base + j * tile, tile)
        return pltpu.make_async_copy(w_ref.at[:, pl.ds(at, tile)], held.at[j], sems.at[j])

    for j in range(tiles):
        fetch(j).start()

    def step(j, carry):
        fetch(j).wait()
        z = jnp.dot(x_ref[...], held[j], preferred_element_type=jnp.float32)
        if out:
            out[0][j] = z
            store(j).start()
        else:
            o_ref[:, pl.ds(pl.multiple_of(j * tile, tile), tile)] = z
        return carry

    def store(j):
        at = pl.ds(pl.multiple_of(j * tile, tile), tile)
        return pltpu.make_async_copy(out[0].at[j], o_ref.at[:, at], out[1].at[j])

    lax.fori_loop(0, tiles, step, 0)
    if out:
        for j in range(tiles):
            store(j).wait()


def project(x, weight, half, keep=False):
    rows, depth = x.shape
    width = weight.shape[1] // 2
    tiles = width // TILE
    scratch = [pltpu.VMEM((tiles, depth, TILE), weight.dtype), pltpu.SemaphoreType.DMA((tiles,))]
    if keep:
        scratch += [pltpu.VMEM((tiles, rows, TILE), jnp.float32), pltpu.SemaphoreType.DMA((tiles,))]
    return kernel(
        project_body,
        pltpu.HBM((rows, width), jnp.float32) if keep else shaped((rows, width), jnp.float32),
        (half, x, in_hbm(weight)),
        (pltpu.SMEM, pltpu.VMEM, pl.ANY),
        scratch,
        pltpu.HBM if keep else pltpu.VMEM,
    )


def back_body(row, half_ref, own_ref, nbr_ref, w_ref, up_ref, mask_ref, *rest):
    o_ref, held, sems, grads, out_sems = rest[-5:]
    tiles, tile, _ = held.shape
    rows, depth = own_ref.shape
    own_at = pl.multiple_of(half_ref[0] * depth, tile)
    nbr_at = pl.multiple_of((1 - half_ref[0]) * depth, tile)
    dims = (((1,), (1,)), ((), ()))
    here = pl.ds(row, rows)

    def fetch(j):
        at = pl.multiple_of(j * tile, tile)
        return pltpu.make_async_copy(w_ref.at[pl.ds(at, tile)], held.at[j], sems.at[j])

    def store(j):
        at = pl.ds(pl.multiple_of(j * tile, tile), tile)
        return pltpu.make_async_copy(grads.at[j], o_ref.at[here, at], out_sems.at[j])

    for j in range(tiles):
        fetch(j).start()

    def step(j, carry):
        fetch(j).wait()
        at = pl.ds(pl.multiple_of(j * tile, tile), tile)
        terms = lax.dot_general(
            own_ref[...], held[j, :, pl.ds(own_at, depth)], dims, preferred_element_type=jnp.float32
        )
        terms += lax.dot_general(
            nbr_ref[...], held[j, :, pl.ds(nbr_at, depth)], dims, preferred_element_type=jnp.float32
        )
        up = up_ref[here, at].astype(jnp.float32)
        grads[j] = ((up + terms) * mask_ref[here, :]).astype(jnp.bfloat16)
        store(j).start()
        return carry

    lax.fori_loop(0, tiles, step, 0)
    for j in range(tiles):
        store(j).wait()


def back_project(own, nbr, weight, half, up, mask, row, before=None):
    width = weight.shape[0]
    tiles = width // TILE
    operands = (half, own, nbr, in_hbm(weight), up, mask)
    spaces = (pltpu.SMEM, pltpu.VMEM, pltpu.VMEM, pl.ANY, pltpu.VMEM, pltpu.VMEM)
    aliases = {}
    if before is not None:
        aliases = {len(operands): 0}
        operands, spaces = operands + (before,), spaces + (pl.ANY,)

    def body(*refs):
        back_body(row, *refs)

    return kernel(
        body,
        pltpu.HBM(up.shape, jnp.bfloat16),
        operands,
        spaces,
        [
            pltpu.VMEM((tiles, TILE, 2 * width), weight.dtype),
            pltpu.SemaphoreType.DMA((tiles,)),
            pltpu.VMEM((tiles, own.shape[0], TILE), jnp.bfloat16),
            pltpu.SemaphoreType.DMA((tiles,)),
        ],
        pltpu.HBM,
        aliases,
    )


def outer_body(other_ref, mine_ref, ga_ref, gb_ref, mask_ref, send_ref, keep_ref, sent, kept, sems):
    tiles, _, tile = kept.shape
    rows = ga_ref.shape[0]

    def store(j, i):
        at = pl.ds(pl.multiple_of(j * tile, tile), tile)
        out, ref = ((sent, send_ref), (kept, keep_ref))[i]
        return pltpu.make_async_copy(out.at[j], ref.at[:, at], sems.at[j, i])

    def step(j, carry):
        at = pl.ds(pl.multiple_of(j * tile, tile), tile)
        ga = (ga_ref[:, at].astype(jnp.float32) * mask_ref[:rows]).astype(jnp.bfloat16)
        gb = (gb_ref[:, at].astype(jnp.float32) * mask_ref[rows:]).astype(jnp.bfloat16)
        for i, lhs, out in ((0, other_ref, sent), (1, mine_ref, kept)):
            total = jnp.dot(lhs[:, :rows], ga, preferred_element_type=jnp.float32)
            total += jnp.dot(lhs[:, rows:], gb, preferred_element_type=jnp.float32)
            out[j] = total.astype(out.dtype)
            store(j, i).start()
        return carry

    lax.fori_loop(0, tiles, step, 0)
    for j in range(tiles):
        for i in range(2):
            store(j, i).wait()


def outer_sum(other, mine, gate_a, gate_b, mask):
    depth, width = other.shape[0], gate_a.shape[1]
    tiles = width // TILE
    return kernel(
        outer_body,
        [pltpu.HBM((depth, width), jnp.bfloat16), pltpu.HBM((depth, width), jnp.float32)],
        (other, mine, gate_a, gate_b, mask),
        (pltpu.VMEM,) * 5,
        [
            pltpu.VMEM((tiles, depth, TILE), jnp.bfloat16),
            pltpu.VMEM((tiles, depth, TILE), jnp.float32),
            pltpu.SemaphoreType.DMA((tiles, 2)),
        ],
        pltpu.HBM,
    )


def pick_body(index_ref, x_ref, o_ref):
    def step(i, carry):
        source = index_ref[i]
        block = x_ref[jnp.maximum(source, 0)]
        o_ref[i] = jnp.where(source >= 0, block, jnp.zeros_like(block))
        return carry

    lax.fori_loop(0, o_ref.shape[0], step, 0)


def pick(index, x):
    shape = shaped((index.shape[0],) + x.shape[1:], x.dtype)
    return kernel(pick_body, shape, (index, x), (pltpu.SMEM, pltpu.VMEM))


def settle_body(x_ref, o_ref):
    pltpu.sync_copy(x_ref, o_ref)


def settle(x):
    return kernel(settle_body, pltpu.HBM(x.shape, x.dtype), (x,), (pltpu.VMEM,), (), pltpu.HBM)


class Order:
    def __init__(self):
        self.last = None

    def tie(self, *arrays):
        if self.last is None:
            return arrays
        return lax.optimization_barrier(arrays + (self.last,))[:-1]

    def mark(self, array):
        self.last = array
        return array

    def here(self, *arrays):
        arrays = self.tie(*arrays)
        self.last = arrays[0]
        return arrays


class Ring:
    def __init__(self, order, keep, send):
        self.order, self.keep = order, keep
        self.got = swap_core(send)
        self.down = self.up = None
        self.next = lax.axis_size("replica") // 4

    def term(self, keep, got, offset, extra):
        chips = lax.axis_size("replica") // 2
        at = (lax.axis_index("replica") // 2 + offset + chips) % chips
        s = lax.dynamic_index_in_dim(keep, at, 0, keepdims=False)
        s = s + lax.dynamic_index_in_dim(got, at, 0, keepdims=False).astype(jnp.float32)
        return s if extra is None else s + extra.astype(jnp.float32)

    def round(self):
        k = self.next
        far = lax.axis_size("replica") // 4
        held = [self.keep, self.got] + [v for v in (self.down, self.up) if v is not None]
        held = list(self.order.tie(*held))
        self.keep, self.got = held[:2]
        cut = self.keep.shape[-1] // 2
        if k == far:
            sent = self.term(self.keep, self.got, k, None).astype(jnp.bfloat16)
            self.order.mark(sent)
            self.down = round_chips(sent[:, :cut], -1)
            self.up = round_chips(sent[:, cut:], 1)
        elif k == 0:
            total = self.term(self.keep, self.got, 0, held[2]) + held[3].astype(jnp.float32)
            return self.order.mark(total)
        else:
            down, up = held[2:]
            if k == far - 1:
                down = jnp.pad(down, ((0, 0), (0, cut)))
                up = jnp.pad(up, ((0, 0), (cut, 0)))
            sent = self.term(self.keep, self.got, -k, down).astype(jnp.bfloat16)
            self.down = round_chips(sent, -1)
            sent = self.term(self.keep, self.got, k, up).astype(jnp.bfloat16)
            self.up = round_chips(sent, 1)
            self.order.mark(sent)
        self.next = k - 1


def local(fresh, counts, wiring, weights, kept, upstream):
    replicas = lax.axis_size("replica")
    chips = replicas // 2
    slots, tokens, width = fresh.shape[2:]
    recv = kept.shape[2]
    cap = recv // replicas
    rows = recv * tokens // 2
    weight = weights[0]
    inputs = fresh[0, 0].reshape(slots * tokens, width)
    stored = kept[0, 0].reshape(2 * rows, width)
    up = upstream[0, 0].reshape(2 * rows, width)
    own = lax.axis_index("tensor").astype(jnp.int32)[None]
    nbr = 1 - own
    core = lax.axis_index("replica") % 2
    order = Order()

    back_nbr = order.mark(project(stored, weight, nbr))

    def send_half(h):
        (x,) = order.tie(back_nbr)
        sent = (x[h * rows : (h + 1) * rows] * Z_SCALE).astype(jnp.float16)
        return swap_tensor(order.mark(sent))

    back_got = [send_half(0)]
    (words,) = order.tie(jnp.concatenate([wiring[0, 0, :, 0], counts[0]])[None])
    plan = shift(order.mark(words), "section", 1)[0]
    back_got.append(send_half(1))

    (x,) = order.tie(stored)
    back_own = order.mark(project(x, weight, own, True))
    (x,) = order.tie(stored)
    turned = x.T.reshape(chips, 2, width // replicas, 2 * rows)
    mine = lax.dynamic_index_in_dim(turned, core, 1, keepdims=False).reshape(width // 2, 2 * rows)
    other = lax.dynamic_index_in_dim(turned, 1 - core, 1, keepdims=False)
    other = order.mark(other.reshape(width // 2, 2 * rows))

    def gate_half(h):
        here = slice(h * rows, (h + 1) * rows)
        z_own, z_got, u = order.tie(back_own, back_got[h], up)
        z = z_own[here] + z_got.astype(jnp.float32) * Z_BACK
        g = jax.nn.sigmoid(z)
        slope = g * (1.0 + z * (1.0 - g))
        return order.mark((u[here].astype(jnp.float32) * slope).astype(jnp.bfloat16))

    def back_half(h, before=None):
        gate, got, u = order.tie(gates[h], gates_nbr[h], up)
        return order.mark(back_project(gate, got, weight, own, u, mask, h * rows, before))

    def across(block):
        return lax.all_to_all(block, "replica", split_axis=0, concat_axis=0, tiled=True)

    def ring_of(first, second):
        first, second = order.tie(first, second)
        send, keep = outer_sum(other, mine, first, second, mask)
        order.mark(keep)
        shape = (chips, width // replicas, width)
        return Ring(order, keep.reshape(shape), send.reshape(shape))

    gates = [gate_half(0)]
    gates_nbr = [swap_tensor(gates[0])]

    (plan,) = order.tie(plan)
    target, count = plan[:slots], plan[slots]
    slot = jnp.arange(slots)
    same = target[:, None] == target[None, :]
    rank = jnp.sum(same & (slot[None, :] < slot[:, None]), axis=1).astype(jnp.int32)
    place = target * cap + rank
    hit = (place[None, :] == jnp.arange(recv)[:, None]) & (slot < count)[None, :]
    source = (jnp.sum(jnp.where(hit, slot[None, :] + 1, 0), axis=1) - 1).astype(jnp.int32)
    flags = order.mark((source >= 0).astype(jnp.bfloat16).reshape(replicas, cap))
    told = across(flags)
    gates.append(gate_half(1))
    gates_nbr.append(swap_tensor(gates[1]))
    (told,) = order.tie(told)
    marks = told.reshape(recv).astype(jnp.float32)
    mask = order.mark(jnp.broadcast_to(marks[:, None], (recv, tokens)).reshape(2 * rows, 1))

    (x,) = order.tie(inputs)
    sent = order.mark((project(x, weight, nbr) * Z_SCALE).astype(jnp.float16))
    forward_got = swap_tensor(sent)
    (x,) = order.tie(inputs)
    forward_own = order.mark(project(x, weight, own, True))

    grads = back_half(0)
    ring_own = ring_of(gates[0], gates[1])
    grads = back_half(1, grads)
    back = across(grads.reshape(replicas, cap, tokens, width))

    forward_own, forward_got, x = order.tie(forward_own, forward_got, inputs)
    forward_z = forward_own + forward_got.astype(jnp.float32) * Z_BACK
    live = (slot < counts[0, 0]).astype(jnp.float32)
    live_rows = jnp.broadcast_to(live[:, None], (slots, tokens)).reshape(slots * tokens, 1)
    outputs = ((x.astype(jnp.float32) + jax.nn.silu(forward_z)) * live_rows).astype(jnp.bfloat16)
    order.mark(outputs)
    outputs = shift(outputs.reshape(slots, tokens, width), "section", 1)

    ring_nbr = ring_of(gates_nbr[0], gates_nbr[1])
    ring_own.round()
    ring_nbr.round()
    (outputs,) = order.tie(outputs)
    packed = order.mark(pick(source, outputs))
    (back,) = order.tie(back)
    returned = order.mark(pick(place, back.reshape(recv, tokens, width)))
    returned = shift(returned, "section", -1)
    sent = order.here(ring_own.down, ring_own.up, ring_nbr.down, ring_nbr.up)
    ring_own.down, ring_own.up, ring_nbr.down, ring_nbr.up = sent
    (packed,) = order.tie(packed)
    arrived = across(packed.reshape(replicas, cap, tokens, width))
    ring_own.round()
    ring_nbr.round()
    ring_own.round()
    ring_nbr.round()
    (x,) = order.tie(returned)
    returned = order.mark(settle(x))
    ring_own.round()
    ring_nbr.round()
    (x,) = order.tie(arrived)
    arrived = order.mark(settle(x))
    sum_own = ring_own.round()
    sum_nbr = ring_nbr.round()
    zero = jnp.zeros((), jnp.int32)
    weight_grad = jnp.zeros((width // replicas, 2 * width), jnp.float32)
    weight_grad = lax.dynamic_update_slice(weight_grad, sum_own, (zero, own[0] * width))
    weight_grad = lax.dynamic_update_slice(weight_grad, sum_nbr, (zero, nbr[0] * width))
    return (
        arrived.reshape(1, 1, recv, tokens, width),
        returned[None, None],
        weight_grad[None],
    )


def solution(mesh):
    placed = (
        P("section", "replica", None, None, "tensor"),
        P("section", "replica"),
        P("section", "replica", None, None),
        P("section", "tensor", None),
        P("section", "replica", None, None, "tensor"),
        P("section", "replica", None, None, "tensor"),
    )
    return jax.shard_map(
        local,
        mesh=mesh,
        in_specs=placed,
        out_specs=(
            P("section", "replica", None, None, "tensor"),
            P("section", "replica", None, None, "tensor"),
            P("section", ("tensor", "replica"), None),
        ),
        check_vma=False,
    )
```
